32 devices in a mesh: seq: 8 (over y, x, core), tp: 4 (over z).
Axes of the slice: x: 2, y: 2, z: 4, core: 2. Of those that a mesh axis runs over, the one named last changes fastest.
Arguments:
- patches: bfloat16 [4096, 1152], P(('seq', 'tp')), may hold values from -6 to 6
- image_patches: int32 [8], P('seq'), may hold values from 385 to 512, as said below
- attn_norm_gain: float32 [1152], replicated, may hold values from 0.1 to 1.9
- attn_norm_shift: float32 [1152], replicated, may hold values from -3 to 3
- query_weight: bfloat16 [1152, 1152], P('seq', 'tp'), may hold values from -0.1875 to 0.1875
- query_bias: float32 [1152], P('tp'), may hold values from -3 to 3
- key_weight: bfloat16 [1152, 1152], P('seq', 'tp'), may hold values from -0.1875 to 0.1875
- value_weight: bfloat16 [1152, 1152], P('seq', 'tp'), may hold values from -0.1875 to 0.1875
- value_bias: float32 [1152], P('tp'), may hold values from -3 to 3
- out_weight: bfloat16 [1152, 1152], P('tp', 'seq'), may hold values from -1 to 1
- out_bias: float32 [1152], replicated, may hold values from -3 to 3
- mlp_norm_gain: float32 [1152], replicated, may hold values from 0.1 to 1.9
- mlp_norm_shift: float32 [1152], replicated, may hold values from -3 to 3
- fc_in_weight: bfloat16 [1152, 4304], P('seq', 'tp'), may hold values from -0.1875 to 0.1875
- fc_in_bias: float32 [4304], P('tp'), may hold values from -3 to 3
- fc_out_weight: bfloat16 [4304, 1152], P('tp', 'seq'), may hold values from -0.125 to 0.125
- fc_out_bias: float32 [1152], replicated, may hold values from -3 to 3
- proj_gate: bfloat16 [1152, 14336], P('seq', 'tp'), may hold values from -0.1875 to 0.1875
- proj_up: bfloat16 [1152, 14336], P('seq', 'tp'), may hold values from -0.1875 to 0.1875
- proj_down: bfloat16 [4096, 14336], P('seq', 'tp'), may hold values from -0.09375 to 0.09375
- latent_param: bfloat16 [64, 4096], P('tp', 'seq'), may hold values from -6 to 6
- context_gain: float32 [4096], replicated, may hold values from 0.1 to 1.9
- latent_gain: float32 [4096], replicated, may hold values from 0.1 to 1.9
- res_query: bfloat16 [4096, 1536], P('seq', 'tp'), may hold values from -0.09375 to 0.09375
- res_key: bfloat16 [4096, 384], P('seq', 'tp'), may hold values from -0.09375 to 0.09375
- res_value: bfloat16 [4096, 384], P('seq', 'tp'), may hold values from -0.09375 to 0.09375
- res_out: bfloat16 [1536, 4096], P('tp', 'seq'), may hold values from -1 to 1
- post_gain: float32 [4096], replicated, may hold values from 0.1 to 1.9
- ffn_gate: bfloat16 [16384, 4096], P(('seq', 'tp')), may hold values from -0.09375 to 0.09375
- ffn_up: bfloat16 [16384, 4096], P(('seq', 'tp')), may hold values from -0.09375 to 0.09375
- ffn_down: bfloat16 [16384, 4096], P(('seq', 'tp')), may hold values from -0.09375 to 0.09375
- cotangent: bfloat16 [512, 4096], P(('seq', 'tp')), may hold values from -6 to 6
Outputs:
- latents: bfloat16 [512, 4096], P(('seq', 'tp'))
- patches_grad: float32 [4096, 1152], P(('seq', 'tp'))
- grad_attn_norm_gain: float32 [1152], replicated
- grad_attn_norm_shift: float32 [1152], replicated
- grad_query_weight: float32 [1152, 1152], P('seq', 'tp')
- grad_query_bias: float32 [1152], P('tp')
- grad_key_weight: float32 [1152, 1152], P('seq', 'tp')
- grad_value_weight: float32 [1152, 1152], P('seq', 'tp')
- grad_value_bias: float32 [1152], P('tp')
- grad_out_weight: float32 [1152, 1152], P('tp', 'seq')
- grad_out_bias: float32 [1152], replicated
- grad_mlp_norm_gain: float32 [1152], replicated
- grad_mlp_norm_shift: float32 [1152], replicated
- grad_fc_in_weight: float32 [1152, 4304], P('seq', 'tp')
- grad_fc_in_bias: float32 [4304], P('tp')
- grad_fc_out_weight: float32 [4304, 1152], P('tp', 'seq')
- grad_fc_out_bias: float32 [1152], replicated
- grad_proj_gate: float32 [1152, 14336], P('seq', 'tp')
- grad_proj_up: float32 [1152, 14336], P('seq', 'tp')
- grad_proj_down: float32 [4096, 14336], P('seq', 'tp')
- grad_latent_param: float32 [64, 4096], P('tp', 'seq')
- grad_context_gain: float32 [4096], replicated
- grad_latent_gain: float32 [4096], replicated
- grad_res_query: float32 [4096, 1536], P('seq', 'tp')
- grad_res_key: float32 [4096, 384], P('seq', 'tp')
- grad_res_value: float32 [4096, 384], P('seq', 'tp')
- grad_res_out: float32 [1536, 4096], P('tp', 'seq')
- grad_post_gain: float32 [4096], replicated
- grad_ffn_gate: float32 [16384, 4096], P(('seq', 'tp'))
- grad_ffn_up: float32 [16384, 4096], P(('seq', 'tp'))
- grad_ffn_down: float32 [16384, 4096], P(('seq', 'tp'))
The draws below stay inside these ranges and needn't reach their ends.
Inputs may be any that keep to these rules, and one draw needn't show every extreme that they name: `image_patches`: valid patches of each image fill its first slots; every image holds more than three quarters of its 512 slots, and some image holds all 512.
All inputs are finite; a program needn't handle non-finite values.
Results may differ from the reference program's by a relative error of at most 0.03.
Values may be sent and summed in bfloat16 or wider, within the bound.
No kernel may reach another device: no remote copies, remote signals or barrier semaphores. Data moves between devices by JAX's collectives and lax.ppermute only.
A program may use at most 640 MiB of HBM per device.

```python
import jax
import jax.numpy as jnp
from jax import lax

D_V = 1152
H_V = 16
HD_V = 72
FF_V = 4304
FF_P = 14336
D = 4096
H_R = 16
KV_R = 4
HD_R = 96
FF_R = 16384
N_LAT = 64
IMG_LEN = 512
IMAGES = 8
PATCHES = 4096
LATENT_ROWS = 512


def draw_image_patches(key, part):
    key = jax.random.fold_in(key, 11)
    count_key, pick_key = jax.random.split(key)
    counts = jax.random.randint(count_key, (IMAGES,), 3 * IMG_LEN // 4 + 1, IMG_LEN + 1)
    chosen = jax.random.randint(pick_key, (), 0, IMAGES)
    return jnp.where(jnp.arange(IMAGES) == chosen, IMG_LEN, counts).astype(jnp.int32)


def block_levels(key, extent, cuts, low, high):
    def one(position, blocks):
        steps = jax.random.uniform(jax.random.fold_in(jax.random.fold_in(key, 6), position), (blocks,), jnp.float32, low / len(cuts), high / len(cuts))
        return jnp.repeat(jnp.exp(steps), extent[position] // blocks).reshape((-1,) + (1,) * (len(extent) - position - 1))

    gain = one(*cuts[0])
    for cut in cuts[1:]:
        gain = gain * one(*cut)
    return gain


def bell_draw(rng, shape, spread, reach, shards=(), kind=jnp.bfloat16):
    result = jax.random.normal(rng, shape, jnp.float32) * spread
    if len(shards) > 0:
        result = block_levels(rng, shape, shards, -0.22, 0.18) * result
    return jnp.clip(result, min=-reach, max=reach).astype(kind)


def setup_inputs(seed: int = 0) -> dict:
    key_of = jax.random.split(jax.random.key(seed), 33)
    patches = bell_draw(key_of[0], (PATCHES, D_V), 1.0, 6.0, ((0, 32),))
    image_patches = draw_image_patches(jax.random.fold_in(key_of[32], 71), 0)
    attn_norm_gain = jnp.clip(1.0 + 0.18 * jax.random.normal(key_of[2], (D_V,), jnp.float32), 0.1, 1.9)
    attn_norm_shift = bell_draw(key_of[3], (D_V,), 0.3, 3.0, (), jnp.float32)
    query_weight = bell_draw(key_of[4], (D_V, D_V), D_V ** -0.5, 0.1875, ((0, 8), (1, 4)))
    query_bias = bell_draw(key_of[5], (D_V,), 0.3, 3.0, ((0, 4),), jnp.float32)
    key_weight = bell_draw(key_of[6], (D_V, D_V), D_V ** -0.5, 0.1875, ((0, 8), (1, 4)))
    value_weight = bell_draw(key_of[7], (D_V, D_V), D_V ** -0.5, 0.1875, ((0, 8), (1, 4)))
    value_bias = bell_draw(key_of[8], (D_V,), 0.3, 3.0, ((0, 4),), jnp.float32)
    out_weight = bell_draw(key_of[9], (D_V, D_V), (max(1, D_V * 16 // IMG_LEN)) ** -0.5, 1.0, ((0, 4), (1, 8)))
    out_bias = bell_draw(key_of[10], (D_V,), 0.3, 3.0, (), jnp.float32)
    mlp_norm_gain = jnp.clip(1.0 + 0.18 * jax.random.normal(key_of[11], (D_V,), jnp.float32), 0.1, 1.9)
    mlp_norm_shift = bell_draw(key_of[12], (D_V,), 0.3, 3.0, (), jnp.float32)
    fc_in_weight = bell_draw(key_of[13], (D_V, FF_V), D_V ** -0.5, 0.1875, ((0, 8), (1, 4)))
    fc_in_bias = bell_draw(key_of[14], (FF_V,), 0.3, 3.0, ((0, 4),), jnp.float32)
    fc_out_weight = bell_draw(key_of[15], (FF_V, D_V), (FF_V // 2) ** -0.5, 0.125, ((0, 4), (1, 8)))
    fc_out_bias = bell_draw(key_of[16], (D_V,), 0.3, 3.0, (), jnp.float32)
    proj_gate = bell_draw(key_of[17], (D_V, FF_P), D_V ** -0.5, 0.1875, ((0, 8), (1, 4)))
    proj_up = bell_draw(key_of[18], (D_V, FF_P), D_V ** -0.5, 0.1875, ((0, 8), (1, 4)))
    proj_down = bell_draw(key_of[19], (D, FF_P), (FF_P // 4) ** -0.5, 0.09375, ((0, 8), (1, 4)))
    latent_param = bell_draw(key_of[20], (N_LAT, D), 1.0, 6.0, ((0, 4), (1, 8)))
    context_gain = jnp.clip(1.0 + 0.18 * jax.random.normal(key_of[21], (D,), jnp.float32), 0.1, 1.9)
    latent_gain = jnp.clip(1.0 + 0.18 * jax.random.normal(key_of[22], (D,), jnp.float32), 0.1, 1.9)
    res_query = bell_draw(key_of[23], (D, H_R * HD_R), D ** -0.5, 0.09375, ((0, 8), (1, 4)))
    res_key = bell_draw(key_of[24], (D, KV_R * HD_R), D ** -0.5, 0.09375, ((0, 8), (1, 4)))
    res_value = bell_draw(key_of[25], (D, KV_R * HD_R), D ** -0.5, 0.09375, ((0, 8), (1, 4)))
    res_out = bell_draw(key_of[26], (H_R * HD_R, D), (max(1, H_R * HD_R * 16 // (IMG_LEN + N_LAT))) ** -0.5, 1.0, ((0, 4), (1, 8)))
    post_gain = jnp.clip(1.0 + 0.18 * jax.random.normal(key_of[27], (D,), jnp.float32), 0.1, 1.9)
    ffn_gate = bell_draw(key_of[28], (FF_R, D), D ** -0.5, 0.09375, ((0, 32),))
    ffn_up = bell_draw(key_of[29], (FF_R, D), D ** -0.5, 0.09375, ((0, 32),))
    ffn_down = bell_draw(key_of[30], (FF_R, D), (FF_R // 4) ** -0.5, 0.09375, ((0, 32),))
    cotangent = bell_draw(key_of[31], (LATENT_ROWS, D), 1.0, 6.0, ((0, 32),))
    return {"patches": patches, "image_patches": image_patches, "attn_norm_gain": attn_norm_gain, "attn_norm_shift": attn_norm_shift, "query_weight": query_weight, "query_bias": query_bias, "key_weight": key_weight, "value_weight": value_weight, "value_bias": value_bias, "out_weight": out_weight, "out_bias": out_bias, "mlp_norm_gain": mlp_norm_gain, "mlp_norm_shift": mlp_norm_shift, "fc_in_weight": fc_in_weight, "fc_in_bias": fc_in_bias, "fc_out_weight": fc_out_weight, "fc_out_bias": fc_out_bias, "proj_gate": proj_gate, "proj_up": proj_up, "proj_down": proj_down, "latent_param": latent_param, "context_gain": context_gain, "latent_gain": latent_gain, "res_query": res_query, "res_key": res_key, "res_value": res_value, "res_out": res_out, "post_gain": post_gain, "ffn_gate": ffn_gate, "ffn_up": ffn_up, "ffn_down": ffn_down, "cotangent": cotangent}


@jax.custom_vjp
def low(v):
    return lax.optimization_barrier(v.astype(jnp.bfloat16)).astype(jnp.float32)

@jax.custom_vjp
def low_back(v):
    return v

def low_keep(v):
    return (low(v), None)

def low_pass(kept, grad):
    return (grad,)

def back_keep(v):
    return (v, None)

def back_low(kept, grad):
    return (low(grad),)
low.defvjp(low_keep, low_pass)
low_back.defvjp(back_keep, back_low)
eps_norm = 1e-06
masked_out = -1e+30
highest = lax.Precision.HIGHEST

def times_exact(left_side, right_side):
    return jnp.dot(left_side, right_side, precision=highest)

def both_ways(inputs):
    return low_back(low(inputs))

def layer_norm(inputs, norm_gain, norm_shift):
    row_mean = lax.optimization_barrier(jnp.mean(inputs, axis=-1, keepdims=True))
    centered = inputs - row_mean
    row_var = lax.optimization_barrier(jnp.mean(centered * centered, axis=-1, keepdims=True))
    return centered * lax.rsqrt(row_var + eps_norm) * norm_gain + norm_shift

def rms_norm(inputs, norm_gain):
    return inputs * lax.rsqrt(lax.optimization_barrier(jnp.mean(inputs * inputs, axis=-1, keepdims=True)) + eps_norm) * norm_gain

def attention(query_rows, key_rows, value_rows, valid_keys, score_scale):
    scores = low_back(jnp.einsum('qcge,kce->cgqk', query_rows, key_rows, precision=highest) * score_scale)
    softmax_weights = jax.nn.softmax(jnp.where(valid_keys, scores, masked_out), axis=-1)
    return both_ways(jnp.einsum('cgqk,kce->qcge', low(softmax_weights), value_rows, precision=highest))

def image_block(params, patch_rows, image_count):
    attn_norm_gain, attn_norm_shift, query_weight, query_bias, key_weight, value_weight, value_bias, out_weight, out_bias, mlp_norm_gain, mlp_norm_shift, fc_in_weight, fc_in_bias, fc_out_weight, fc_out_bias, proj_gate, proj_up, proj_down, latent_param, context_gain, latent_gain, res_query, res_key, res_value, res_out, post_gain, ffn_gate, ffn_up, ffn_down = params
    row_valid = jnp.arange(IMG_LEN) < image_count
    norm_one = low(layer_norm(patch_rows, attn_norm_gain, attn_norm_shift))
    query_rows = both_ways(times_exact(norm_one, query_weight) + query_bias).reshape(IMG_LEN, H_V, 1, HD_V)
    key_rows = both_ways(times_exact(norm_one, key_weight)).reshape(IMG_LEN, H_V, HD_V)
    value_rows = both_ways(times_exact(norm_one, value_weight) + value_bias).reshape(IMG_LEN, H_V, HD_V)
    attended = attention(query_rows, key_rows, value_rows, row_valid[None, None, None, :], HD_V ** (-0.5))
    attended = attended.reshape(IMG_LEN, D_V)
    after_attn = patch_rows + low_back(times_exact(attended, out_weight)) + out_bias
    norm_two = low(layer_norm(after_attn, mlp_norm_gain, mlp_norm_shift))
    fc_pre = low_back(times_exact(norm_two, fc_in_weight) + fc_in_bias)
    fc_act = low(jax.nn.gelu(fc_pre, approximate=True))
    vis_out = after_attn + low_back(times_exact(fc_act, fc_out_weight)) + fc_out_bias
    vis_low = low(vis_out)
    gate_pre = low_back(times_exact(vis_low, proj_gate))
    up_pre = low_back(times_exact(vis_low, proj_up))
    hidden = low(jax.nn.silu(gate_pre) * up_pre)
    context = low_back(times_exact(hidden, proj_down.T))
    ctx_norm = low(rms_norm(context, context_gain))
    lat_norm = low(rms_norm(latent_param, latent_gain))
    kv_input = jnp.concatenate([ctx_norm, lat_norm], axis=0)
    group_size = H_R // KV_R
    res_queries = both_ways(times_exact(lat_norm, res_query)).reshape(N_LAT, KV_R, group_size, HD_R)
    res_keys = both_ways(times_exact(kv_input, res_key)).reshape(IMG_LEN + N_LAT, KV_R, HD_R)
    res_values = both_ways(times_exact(kv_input, res_value)).reshape(IMG_LEN + N_LAT, KV_R, HD_R)
    res_valid = jnp.concatenate([row_valid, jnp.ones((N_LAT,), jnp.bool_)])
    res_mixed = attention(res_queries, res_keys, res_values, res_valid[None, None, None, :], HD_R ** (-0.5))
    res_mixed = res_mixed.reshape(N_LAT, H_R * HD_R)
    lat_after = latent_param + low_back(times_exact(res_mixed, res_out))
    post_norm = low(rms_norm(lat_after, post_gain))
    ffn_gate_pre = low_back(times_exact(post_norm, ffn_gate.T))
    ffn_up_pre = low_back(times_exact(post_norm, ffn_up.T))
    ffn_hidden = low(jax.nn.silu(ffn_gate_pre) * ffn_up_pre)
    return lat_after + times_exact(ffn_hidden, ffn_down)

def reference(patches, image_patches, attn_norm_gain, attn_norm_shift, query_weight, query_bias, key_weight, value_weight, value_bias, out_weight, out_bias, mlp_norm_gain, mlp_norm_shift, fc_in_weight, fc_in_bias, fc_out_weight, fc_out_bias, proj_gate, proj_up, proj_down, latent_param, context_gain, latent_gain, res_query, res_key, res_value, res_out, post_gain, ffn_gate, ffn_up, ffn_down, cotangent):
    params = tuple((member.astype(jnp.float32) for member in (attn_norm_gain, attn_norm_shift, query_weight, query_bias, key_weight, value_weight, value_bias, out_weight, out_bias, mlp_norm_gain, mlp_norm_shift, fc_in_weight, fc_in_bias, fc_out_weight, fc_out_bias, proj_gate, proj_up, proj_down, latent_param, context_gain, latent_gain, res_query, res_key, res_value, res_out, post_gain, ffn_gate, ffn_up, ffn_down)))
    patch_rows = patches.astype(jnp.float32).reshape(IMAGES, IMG_LEN, D_V)
    grad_rows = cotangent.astype(jnp.float32).reshape(IMAGES, N_LAT, D)

    def forward(all_rows, weights):

        def one_image(image_item):
            return image_block(weights, image_item[0], image_item[1])
        return lax.map(jax.checkpoint(one_image), (all_rows, image_patches))
    outputs, pull_back = jax.vjp(forward, patch_rows, params)
    grad_patches, grad_params = pull_back(grad_rows)
    grad_attn_norm_gain, grad_attn_norm_shift, grad_query_weight, grad_query_bias, grad_key_weight, grad_value_weight, grad_value_bias, grad_out_weight, grad_out_bias, grad_mlp_norm_gain, grad_mlp_norm_shift, grad_fc_in_weight, grad_fc_in_bias, grad_fc_out_weight, grad_fc_out_bias, grad_proj_gate, grad_proj_up, grad_proj_down, grad_latent_param, grad_context_gain, grad_latent_gain, grad_res_query, grad_res_key, grad_res_value, grad_res_out, grad_post_gain, grad_ffn_gate, grad_ffn_up, grad_ffn_down = grad_params
    return (outputs.reshape(IMAGES * N_LAT, D).astype(jnp.bfloat16), grad_patches.reshape(IMAGES * IMG_LEN, D_V), grad_attn_norm_gain, grad_attn_norm_shift, grad_query_weight, grad_query_bias, grad_key_weight, grad_value_weight, grad_value_bias, grad_out_weight, grad_out_bias, grad_mlp_norm_gain, grad_mlp_norm_shift, grad_fc_in_weight, grad_fc_in_bias, grad_fc_out_weight, grad_fc_out_bias, grad_proj_gate, grad_proj_up, grad_proj_down, grad_latent_param, grad_context_gain, grad_latent_gain, grad_res_query, grad_res_key, grad_res_value, grad_res_out, grad_post_gain, grad_ffn_gate, grad_ffn_up, grad_ffn_down)
```

```python
import functools

import jax
import jax.numpy as jnp
from jax import lax
from jax.experimental import pallas as pl
from jax.experimental.pallas import tpu as pltpu
from jax.sharding import PartitionSpec as P

HD_V = 72
H_R = 16
KV_R = 4
HD_R = 96


eps_norm = 1e-06
masked_out = -1e30


def as_sent(value):
    return jax.tree.map(lambda a: a.astype(jnp.bfloat16) if a.dtype == jnp.float32 else a, value)


def layer_norm(inputs, norm_gain, norm_shift):
    row_mean = jnp.mean(inputs, axis=-1, keepdims=True)
    centered = inputs - row_mean
    row_var = jnp.mean(centered * centered, axis=-1, keepdims=True)
    return centered * lax.rsqrt(row_var + eps_norm) * norm_gain + norm_shift


def rms_norm(inputs, norm_gain):
    return (
        inputs * lax.rsqrt(jnp.mean(inputs * inputs, axis=-1, keepdims=True) + eps_norm) * norm_gain
    )


def gelu_tanh(inputs):
    return jax.nn.gelu(inputs, approximate=True)


def swish_gate(gate_pre, up_pre):
    return jax.nn.silu(gate_pre) * up_pre


def swish_back(gate_pre, up_pre, grad_hidden):
    ignored, pull_back = jax.vjp(swish_gate, gate_pre, up_pre)
    grad_gate, grad_up = pull_back(grad_hidden)
    return (grad_gate.astype(jnp.bfloat16), grad_up.astype(jnp.bfloat16))


def times_plain(left_side, right_side):
    return jnp.dot(left_side, right_side, preferred_element_type=jnp.float32)


def times_left(left_side, right_side):
    return lax.dot_general(
        left_side, right_side, (((0,), (0,)), ((), ())), preferred_element_type=jnp.float32
    )


def times_right(left_side, right_side):
    return lax.dot_general(
        left_side, right_side, (((1,), (1,)), ((), ())), preferred_element_type=jnp.float32
    )


def attend(query_rows, key_rows, value_rows, valid_keys, score_scale):
    scores = (
        jnp.einsum("qcge,kce->cgqk", query_rows, key_rows, preferred_element_type=jnp.float32)
        * score_scale
    )
    scores = jnp.where(valid_keys, scores, masked_out)
    top_score = jnp.max(scores, axis=-1, keepdims=True)
    total = jnp.sum(jnp.exp(scores - top_score), axis=-1, keepdims=True)
    log_total = top_score + jnp.log(total)
    weights = jnp.exp(scores - log_total).astype(jnp.bfloat16)
    mixed_rows = jnp.einsum(
        "cgqk,kce->qcge", weights, value_rows, preferred_element_type=jnp.float32
    )
    return (mixed_rows.astype(jnp.bfloat16), log_total)


def attend_back(query_rows, key_rows, value_rows, valid_keys, score_scale, log_total, grad_mixed):
    scores = (
        jnp.einsum("qcge,kce->cgqk", query_rows, key_rows, preferred_element_type=jnp.float32)
        * score_scale
    )
    scores = jnp.where(valid_keys, scores, masked_out)
    probs_full = jnp.exp(scores - log_total)
    grad_probs = jnp.einsum(
        "qcge,kce->cgqk", grad_mixed, value_rows, preferred_element_type=jnp.float32
    )
    inner_sum = jnp.sum(probs_full * grad_probs, axis=-1, keepdims=True)
    grad_scores = (probs_full * (grad_probs - inner_sum)).astype(jnp.bfloat16)
    grad_query = (
        jnp.einsum("cgqk,kce->qcge", grad_scores, key_rows, preferred_element_type=jnp.float32)
        * score_scale
    ).astype(jnp.bfloat16)
    grad_key = (
        jnp.einsum("cgqk,qcge->kce", grad_scores, query_rows, preferred_element_type=jnp.float32)
        * score_scale
    ).astype(jnp.bfloat16)
    grad_value = jnp.einsum(
        "cgqk,qcge->kce",
        probs_full.astype(jnp.bfloat16),
        grad_mixed,
        preferred_element_type=jnp.float32,
    ).astype(jnp.bfloat16)
    return (grad_query, grad_key, grad_value)


def bits_of(count):
    return [1 << i for i in range(count.bit_length() - 1)]


def swap(value, bit, axis, count):
    return lax.ppermute(value, axis, [(i, i ^ bit) for i in range(count)])


def tie(*values):
    return lax.optimization_barrier(values)


def tp_gather(rows_in, count):
    held = {0: rows_in}
    for bit in bits_of(count)[::-1]:
        for j in sorted(held):
            held[j ^ bit] = swap(held[j], bit, "tp", count)
    return [held[j] for j in range(count)]


def tp_scatter(part_of, count):
    parts = {}
    for j in range(count - 1, -1, -1):
        parts[j] = part_of(j)
    for bit in bits_of(count):
        for j in sorted(parts, reverse=True):
            if j & bit:
                parts[j ^ bit] = parts[j ^ bit].astype(jnp.float32) + swap(
                    parts.pop(j).astype(jnp.bfloat16), bit, "tp", count
                ).astype(jnp.float32)
    return parts[0]


def tp_direct(parts, count):
    return [parts[0]] + [swap(parts[j], j, "tp", count) for j in range(1, count)]


def tp_direct_sum(parts, count):
    total = parts[0].astype(jnp.float32)
    for got in tp_direct([parts[0]] + [p.astype(jnp.bfloat16) for p in parts[1:]], count)[1:]:
        total = total + got.astype(jnp.float32)
    return total


def split_orders(count):
    bits = bits_of(count)
    return bits[1:] + bits[:1], bits[:0:-1] + bits[:1]


def swap_each(block_of, count):
    return [block_of(0)] + [swap(block_of(k), k, "seq", count) for k in range(1, count)]


def gather_seq(block, axis=0):
    return lax.all_gather(block, "seq", axis=axis, tiled=True)


def scatter_seq(terms, axis=0):
    return lax.psum_scatter(terms.astype(jnp.bfloat16), "seq", scatter_dimension=axis, tiled=True)


def sum_seq(value, count):
    for bit in bits_of(count):
        value = value + swap(value, bit, "seq", count)
    return value


def add_products(places, rows, *refs):
    lefts, rights, total = refs[: -len(places) - 1], refs[-len(places) - 1 : -1], None
    for (place, part), right in zip(places, rights):
        left = lefts[place][:, part * rows : (part + 1) * rows]
        term = jnp.dot(left, right[...], preferred_element_type=jnp.float32)
        total = term if total is None else total + term
    refs[-1][...] = total


def sum_of_products(lefts, rights, places, tile=512):
    height, rows, width = lefts[0].shape[0], rights[0].shape[0], rights[0].shape[1]
    return pl.pallas_call(
        functools.partial(add_products, places, rows),
        grid=(width // tile,),
        in_specs=[pl.BlockSpec(left.shape, lambda n: (0, 0)) for left in lefts]
        + [pl.BlockSpec((rows, tile), lambda n: (0, n)) for right in rights],
        out_specs=pl.BlockSpec((height, tile), lambda n: (0, n)),
        out_shape=jax.ShapeDtypeStruct((height, width), jnp.float32),
        compiler_params=pltpu.CompilerParams(vmem_limit_bytes=48 * 1024 * 1024),
        cost_estimate=pl.CostEstimate(
            flops=2 * height * rows * width * len(rights),
            bytes_accessed=2 * rows * width * len(rights) + 4 * height * width,
            transcendentals=0,
        ),
    )(*lefts, *rights)


def sum_every(vector, tensor):
    size = vector.shape[0]
    table = jnp.pad(vector, (0, -size % 1024)).reshape(-1, 128)
    for bit in bits_of(tensor):
        table = table + swap(table, bit, "tp", tensor)
    every = lax.all_gather(table, "seq", axis=0, tiled=True)
    return jnp.sum(every.reshape((-1,) + table.shape), axis=0).reshape(-1)[:size]


def pad_cols(value, unit=128):
    spare = -value.shape[1] % unit
    return jnp.pad(value, ((0, 0), (0, spare))) if spare else value


def spread_slot(vector, tensor, tp_index):
    whole_vec = jnp.zeros((vector.shape[0] * tensor,), jnp.float32)
    return lax.dynamic_update_slice_in_dim(whole_vec, vector, tp_index * vector.shape[0], 0)


def take_slot(vector, tensor, tp_index):
    slot_width = vector.shape[0] // tensor
    return lax.dynamic_slice_in_dim(vector, tp_index * slot_width, slot_width, 0)


def shards(
    patches,
    image_patches,
    attn_norm_gain,
    attn_norm_shift,
    query_weight,
    query_bias,
    key_weight,
    value_weight,
    value_bias,
    out_weight,
    out_bias,
    mlp_norm_gain,
    mlp_norm_shift,
    fc_in_weight,
    fc_in_bias,
    fc_out_weight,
    fc_out_bias,
    proj_gate,
    proj_up,
    proj_down,
    latent_param,
    context_gain,
    latent_gain,
    res_query,
    res_key,
    res_value,
    res_out,
    post_gain,
    ffn_gate,
    ffn_up,
    ffn_down,
    cotangent,
):
    tensor = lax.axis_size("tp")
    count = lax.axis_size("seq")
    tp_index = lax.axis_index("tp")
    seq_index = lax.axis_index("seq")
    bf16, f32 = jnp.bfloat16, jnp.float32
    own_rows = patches.shape[0]
    seq_len = own_rows * tensor
    chunks = range(tensor)
    row_ids = jnp.concatenate([(tp_index ^ j) * own_rows + jnp.arange(own_rows) for j in chunks])
    row_valid = row_ids < image_patches[0]
    vis_valid = row_valid[None, None, None, :]
    vis_heads = query_weight.shape[1] // HD_V
    head_width = vis_heads * HD_V
    fc_width = fc_in_weight.shape[1]
    group_size = H_R // KV_R
    vis_scale = HD_V ** (-0.5)
    res_scale = HD_R ** (-0.5)
    d_vis = patches.shape[1]
    d_text = cotangent.shape[1]
    own_cols = latent_param.shape[1]

    def rows_of(value, j):
        return value[j * own_rows : (j + 1) * own_rows]

    proj_width = proj_gate.shape[1]
    owned = [
        proj_gate,
        proj_up,
        pad_cols(jnp.concatenate([query_weight, key_weight, value_weight], axis=1)),
        pad_cols(out_weight.T),
        pad_cols(fc_in_weight),
        pad_cols(fc_out_weight.T),
    ]
    narrow_full = gather_seq(jnp.concatenate(owned, axis=1))
    pdown_full = gather_seq(proj_down)
    starts = [0]
    for block in owned:
        starts.append(starts[-1] + block.shape[1])
    lat_rows = lax.all_gather(latent_param, "seq", axis=1, tiled=True).astype(f32)
    lat_r = lax.rsqrt(jnp.mean(lat_rows * lat_rows, axis=-1, keepdims=True) + eps_norm)
    latent_gain_own = lax.dynamic_slice_in_dim(latent_gain, seq_index * own_cols, own_cols, 0)
    lat_own = latent_param.astype(f32)
    lat_norm_own = (lat_own * lat_r * latent_gain_own).astype(bf16)
    lat_norm_own = jnp.concatenate(tp_direct([lat_norm_own] * tensor, tensor), axis=0)
    latent_rows = latent_param.shape[0]
    latent_count = lat_norm_own.shape[0]
    rkv_own = jnp.concatenate([res_key, res_value], axis=1)
    rkv_width = rkv_own.shape[1]
    res_own = jnp.concatenate([res_query, rkv_own], axis=1)
    query_width = res_query.shape[1]
    lat_proj_sum = sum_seq(times_plain(lat_norm_own, res_own), count)
    rkv_heads = jnp.concatenate(tp_direct([rkv_own] * tensor, tensor), axis=1)
    cot_rows = jnp.concatenate(tp_direct([cotangent] * tensor, tensor), axis=0)
    narrow_full, lat_proj_sum, rkv_heads, cot_rows = tie(
        narrow_full, lat_proj_sum, rkv_heads, cot_rows
    )
    lat_proj = lat_proj_sum.astype(bf16)

    pair_full = narrow_full[:, : 2 * proj_width]
    qkv_full = narrow_full[:, starts[2] : starts[2] + 3 * head_width]
    out_full = narrow_full[:, starts[3] : starts[3] + head_width]
    fc_in_full = narrow_full[:, starts[4] : starts[4] + fc_width]
    fc_out_full = narrow_full[:, starts[5] : starts[5] + fc_width]

    patch_rows = patches.astype(f32)

    norm_one = layer_norm(patch_rows, attn_norm_gain, attn_norm_shift).astype(bf16)
    norm_all = jnp.concatenate(tp_gather(norm_one, tensor), axis=0)
    qkv_bias = jnp.concatenate([query_bias, jnp.zeros_like(query_bias), value_bias])
    qkv_rows = (times_plain(norm_all, qkv_full) + qkv_bias).astype(bf16)
    query_rows = qkv_rows[:, :head_width].reshape(seq_len, vis_heads, 1, HD_V)
    key_rows = qkv_rows[:, head_width : 2 * head_width].reshape(seq_len, vis_heads, HD_V)
    value_rows = qkv_rows[:, 2 * head_width :].reshape(seq_len, vis_heads, HD_V)
    attended, vis_total = attend(query_rows, key_rows, value_rows, vis_valid, vis_scale)
    attended = attended.reshape(seq_len, head_width)
    attn_sum = tp_scatter(lambda j: times_right(rows_of(attended, j), out_full), tensor)
    after_attn = patch_rows + attn_sum + out_bias
    norm_two = tp_gather(layer_norm(after_attn, mlp_norm_gain, mlp_norm_shift).astype(bf16), tensor)
    fc_pre = [times_plain(norm_two[j], fc_in_full) + fc_in_bias for j in chunks]
    fc_act = [gelu_tanh(fc_pre[j]).astype(bf16) for j in chunks]
    fc_sum = tp_direct_sum([times_right(fc_act[j], fc_out_full) for j in chunks], tensor)
    vis_out = after_attn + fc_sum + fc_out_bias
    vis_rows = tp_gather(vis_out.astype(bf16), tensor)

    vis_all = jnp.concatenate(vis_rows, axis=0)
    pair_pre = times_plain(vis_all, pair_full)
    gate_pre, up_pre = pair_pre[:, :proj_width], pair_pre[:, proj_width:]
    hidden_all = swish_gate(gate_pre, up_pre).astype(bf16)

    hidden_all, rkv_heads, ro_late, cot_rows = tie(hidden_all, rkv_heads, res_out, cot_rows)
    rkv_full = gather_seq(rkv_heads)
    ro_full = gather_seq(ro_late, 1)
    cot_every = gather_seq(cot_rows)

    group = d_text // 4
    context = []
    for g in range(4):
        terms = times_right(hidden_all, pdown_full[g * group : (g + 1) * group]).astype(bf16)
        context.append(tp_scatter(lambda j: rows_of(terms, j), tensor))
    context = jnp.concatenate(context, axis=1)

    ctx_norm = rms_norm(context, context_gain).astype(bf16)
    kv_own = times_plain(ctx_norm, rkv_full).astype(bf16)
    kv_image = jnp.concatenate(
        tp_direct([kv_own[:, j * rkv_width : (j + 1) * rkv_width] for j in chunks], tensor), axis=0
    )
    kv_rows = jnp.concatenate([kv_image, lat_proj[:, query_width:]], axis=0)
    res_valid = jnp.concatenate([row_valid, jnp.ones((latent_count,), jnp.bool_)])[
        None, None, None, :
    ]
    kv_local = res_key.shape[1] // HD_R
    res_queries = lat_proj[:, :query_width].reshape(latent_count, kv_local, group_size, HD_R)
    res_keys = kv_rows[:, : kv_local * HD_R].reshape(-1, kv_local, HD_R)
    res_values = kv_rows[:, kv_local * HD_R :].reshape(-1, kv_local, HD_R)
    res_mixed, res_total = attend(res_queries, res_keys, res_values, res_valid, res_scale)
    res_mixed = res_mixed.reshape(latent_count, query_width)
    mixed_out = times_plain(res_mixed, ro_full)
    lat_after = lat_rows + tp_direct_sum(
        [mixed_out[j * latent_rows : (j + 1) * latent_rows] for j in chunks], tensor
    )
    post_norm = rms_norm(lat_after, post_gain).astype(bf16)

    post_norm, cot_every = tie(post_norm, cot_every)
    ffn_input = gather_seq(jnp.concatenate(tp_direct([post_norm] * tensor, tensor), axis=0))
    grad_fhidden = times_right(cot_every, ffn_down)
    half = seq_len // 2
    hidden_held = [hidden_all[:half], hidden_all[half:]]
    if count == 8:
        low_bits, high_bits = split_orders(count)
        ffn_input, *hidden_held = tie(ffn_input, *hidden_held)
        ways = (low_bits, high_bits)
        hidden_got = [swap(h, w[0], "seq", count) for h, w in zip(hidden_held, ways)]
    ffn_gate_pre = times_right(ffn_input, ffn_gate)
    ffn_up_pre = times_right(ffn_input, ffn_up)
    grad_fgate, grad_fup = swish_back(ffn_gate_pre, ffn_up_pre, grad_fhidden)
    latent_chunks = [slice(j * latent_rows, (j + 1) * latent_rows) for j in chunks]

    def rows_home(mine):
        return tp_direct_sum([mine[rows] for rows in latent_chunks], tensor)

    post_sum = scatter_seq(times_plain(grad_fgate, ffn_gate) + times_plain(grad_fup, ffn_up))
    ffn_hidden = swish_gate(ffn_gate_pre, ffn_up_pre).astype(bf16)
    grad_ffn_down = times_left(ffn_hidden, cot_every)
    grad_ffn_gate = times_left(grad_fgate, ffn_input)
    grad_ffn_up = times_left(grad_fup, ffn_input)
    ffn_hidden_late = ffn_hidden
    if count == 8:
        ffn_hidden_late, *hidden_got = tie(ffn_hidden, *hidden_got)
    ffn_terms = times_plain(ffn_hidden_late, ffn_down).astype(bf16)
    post_sum, grad_ffn_down, grad_ffn_gate, grad_ffn_up, ffn_terms = tie(
        post_sum, grad_ffn_down, grad_ffn_gate, grad_ffn_up, ffn_terms
    )
    ffn_sum = scatter_seq(ffn_terms)
    grad_post = rows_home(post_sum)
    ignored, pull_post = jax.vjp(rms_norm, lat_after, post_gain)
    grad_lat_post, grad_post_gain = pull_post(grad_post)
    grad_after = cotangent.astype(f32) + grad_lat_post
    grad_after_all = jnp.concatenate(
        tp_direct([grad_after.astype(bf16)] * tensor, tensor), axis=0
    )
    grad_rmixed = (
        times_right(grad_after_all, ro_full)
        .astype(bf16)
        .reshape(latent_count, kv_local, group_size, HD_R)
    )
    grad_rq, grad_rk, grad_rv = attend_back(
        res_queries, res_keys, res_values, res_valid, res_scale, res_total, grad_rmixed
    )
    grad_kv = jnp.concatenate(
        [grad_rk.reshape(-1, kv_local * HD_R), grad_rv.reshape(-1, kv_local * HD_R)], axis=1
    )
    grad_kv_own = jnp.concatenate(
        tp_direct([rows_of(grad_kv, j) for j in chunks], tensor), axis=1
    )
    if count == 8:
        grad_kv_own, hidden_held, hidden_got = tie(grad_kv_own, hidden_held, hidden_got)
        hidden_far = [
            swap(h, w[1], "seq", count) for hs in (hidden_held, hidden_got) for h, w in zip(hs, ways)
        ]
    grad_ctx_norm = times_right(grad_kv_own, rkv_full)
    ignored, pull_ctx = jax.vjp(rms_norm, context, context_gain)
    grad_context, grad_context_gain = pull_ctx(grad_ctx_norm)

    grad_ctx = tp_gather(grad_context.astype(bf16), tensor)
    grad_rkv_ctx = scatter_seq(times_left(ctx_norm, grad_kv_own))
    both_every = gather_seq(jnp.concatenate([grad_after_all, res_mixed], axis=1))
    if count == 8:
        grad_ctx[2], *hidden_far[:2] = tie(grad_ctx[2], *hidden_far[:2])
    if count == 8:
        grad_ctx_turned = jnp.concatenate(grad_ctx, axis=0).T
        ctx_held = swap_each(
            lambda k: lax.dynamic_slice_in_dim(
                grad_ctx_turned, (seq_index ^ k) * own_cols, own_cols, 0
            ),
            count,
        )
    grad_pair, vis_parts = [], []
    steps = [chunks[i : i + 2] for i in range(0, tensor, 2)]
    for step in steps:
        rows = slice(step[0] * own_rows, (step[-1] + 1) * own_rows)
        grad_phidden = times_plain(
            jnp.concatenate([grad_ctx[j] for j in step], axis=0), pdown_full
        )
        grad_pair.append(
            jnp.concatenate(swish_back(gate_pre[rows], up_pre[rows], grad_phidden), axis=1)
        )
        if count == 8 and step is steps[-1]:
            grad_pair[-1], *ctx_held = tie(grad_pair[-1], *ctx_held)
        terms = times_right(grad_pair[-1], pair_full)
        vis_parts += [rows_of(terms, i) for i in range(len(step))]
    grad_vis = tp_direct_sum(vis_parts, tensor)
    grad_pair_sum = scatter_seq(times_left(vis_all, jnp.concatenate(grad_pair, axis=0)))
    grad_ctx_all = jnp.concatenate(grad_ctx, axis=0)

    grad_fc_out_rows = jnp.sum(grad_vis, axis=0)
    grad_vis, ffn_sum, grad_rkv_ctx, both_every = tie(grad_vis, ffn_sum, grad_rkv_ctx, both_every)
    if count == 8:
        grad_vis, *hidden_far[2:] = tie(grad_vis, *hidden_far[2:])
    grad_vis_rows = tp_gather(grad_vis.astype(bf16), tensor)
    grad_fc_pre = []
    for j in chunks:
        ignored, pull_gelu = jax.vjp(gelu_tanh, fc_pre[j])
        grad_fc_pre.append(pull_gelu(times_plain(grad_vis_rows[j], fc_out_full))[0].astype(bf16))
    grad_norm_two = tp_direct_sum([times_right(g, fc_in_full) for g in grad_fc_pre], tensor)
    grad_norm_two, grad_fc_late, grad_vis_late = tie(
        grad_norm_two, jnp.concatenate(grad_fc_pre, axis=0), jnp.concatenate(grad_vis_rows, axis=0)
    )
    if count == 8:
        hidden_held = hidden_held + hidden_got + hidden_far
        hidden_held = hidden_held + [swap(h, 1, "seq", count) for h in hidden_held]
    ignored, pull_two = jax.vjp(layer_norm, after_attn, mlp_norm_gain, mlp_norm_shift)
    grad_mid_norm, grad_mlp_gain, grad_mlp_shift = pull_two(grad_norm_two)
    grad_mid = grad_vis + grad_mid_norm
    grad_out_rows = jnp.sum(grad_mid, axis=0)
    grad_mid_all = jnp.concatenate(tp_gather(grad_mid.astype(bf16), tensor), axis=0)
    fc_in_sum = scatter_seq(times_left(jnp.concatenate(norm_two, axis=0), grad_fc_late))
    fc_out_sum = scatter_seq(times_left(grad_vis_late, jnp.concatenate(fc_act, axis=0)))
    grad_attended = (
        times_plain(grad_mid_all, out_full).astype(bf16).reshape(seq_len, vis_heads, 1, HD_V)
    )
    out_sum = scatter_seq(times_left(grad_mid_all, attended))
    grad_vq, grad_vk, grad_vv = attend_back(
        query_rows, key_rows, value_rows, vis_valid, vis_scale, vis_total, grad_attended
    )
    grad_qkv = jnp.concatenate(
        [g.reshape(seq_len, head_width) for g in (grad_vq, grad_vk, grad_vv)], axis=1
    )
    grad_lat_own = jnp.concatenate(
        [grad_rq.reshape(latent_count, query_width), grad_kv[seq_len:]], axis=1
    )
    grad_qkv, grad_lat_own, grad_rkv_ctx, ffn_sum, grad_pair_sum = tie(
        grad_qkv, grad_lat_own, grad_rkv_ctx, ffn_sum, grad_pair_sum
    )
    after_every = lax.dynamic_slice_in_dim(both_every, seq_index * own_cols, own_cols, 1)
    grad_res_out = times_left(both_every[:, d_text:], after_every)
    after_own = lax.dynamic_slice_in_dim(
        both_every[:, :d_text].reshape(count, latent_count, d_text),
        seq_index * own_cols,
        own_cols,
        2,
    )[:, :latent_rows]
    grad_after_sum = jnp.sum(after_own.astype(f32), axis=0)
    grad_lat_sum = jnp.sum(
        lax.all_gather(grad_lat_own, "seq", axis=0).astype(f32), axis=0
    )
    grad_lat_proj = grad_lat_sum.astype(bf16)
    grad_res = times_left(lat_norm_own, grad_lat_proj)
    grad_res_query = grad_res[:, :query_width]
    grad_lat_terms = jnp.concatenate(
        [
            times_right(grad_lat_proj, res_own),
            jnp.broadcast_to(
                jnp.sum(grad_lat_proj.astype(f32) * lat_proj_sum, axis=-1, keepdims=True),
                (latent_count, 128),
            ),
        ],
        axis=1,
    )
    lat_each = tp_direct([grad_lat_terms[rows] for rows in latent_chunks], tensor)
    grad_lat_norm = sum(lat_each[1:], lat_each[0])
    lat_inner = grad_lat_norm[:, own_cols : own_cols + 1] / lat_r
    grad_lat_norm = grad_lat_norm[:, :own_cols]
    grad_lat_rows = (
        lat_r * latent_gain_own * grad_lat_norm - lat_own * lat_r**3 * lat_inner / d_text
    )
    grad_latent_gain = jnp.sum(grad_lat_norm * lat_own * lat_r, axis=0)
    grad_latent_param = grad_lat_rows + grad_after_sum

    grad_rkv_ctx = tp_direct_sum(
        [grad_rkv_ctx[:, j * rkv_width : (j + 1) * rkv_width] for j in chunks], tensor
    )
    grad_rkv = grad_res[:, query_width:] + grad_rkv_ctx
    grad_res_key = grad_rkv[:, : kv_local * HD_R]
    grad_res_value = grad_rkv[:, kv_local * HD_R :]
    latents = (lat_after + rows_home(ffn_sum)).astype(bf16)
    if count == 8:
        grad_qkv, *hidden_held = tie(grad_qkv, *hidden_held)
        places = []
        for core in (0, 1):
            for step in (lambda w: 0, lambda w: w[0], lambda w: w[1], lambda w: w[0] ^ w[1]):
                places += [(step(w) ^ core, f) for f, w in enumerate(ways)]
        grad_proj_down = sum_of_products(ctx_held, hidden_held, places)
    else:
        grad_proj_down = scatter_seq(times_left(grad_ctx_all, hidden_all)).astype(f32)
    qkv_sum = scatter_seq(times_left(norm_all, grad_qkv))
    grad_norm_one = tp_scatter(lambda j: times_right(rows_of(grad_qkv, j), qkv_full), tensor)
    grad_fc_in_part = jnp.sum(grad_fc_late.astype(f32), axis=0)

    def sum_pieces(pieces):
        summed = sum_every(jnp.concatenate(pieces), tensor)
        sums, start = [], 0
        for piece in pieces:
            sums.append(summed[start : start + piece.shape[0]])
            start += piece.shape[0]
        return sums

    grad_norm_one, fc_in_sum, fc_out_sum = tie(grad_norm_one, fc_in_sum, fc_out_sum)
    grad_bias_part = jnp.sum(grad_qkv.astype(f32), axis=0)
    ignored, pull_one = jax.vjp(layer_norm, patch_rows, attn_norm_gain, attn_norm_shift)
    grad_in_norm, grad_attn_gain, grad_attn_shift = pull_one(grad_norm_one)
    patches_grad = grad_mid + grad_in_norm

    patches_grad, fc_in_sum, fc_out_sum, out_sum, qkv_sum = tie(
        patches_grad, fc_in_sum, fc_out_sum, out_sum, qkv_sum
    )
    grad_qkv_sum, grad_out = qkv_sum.astype(f32), out_sum.T.astype(f32)
    grad_fc_in, grad_fc_out = fc_in_sum.astype(f32), fc_out_sum.T.astype(f32)
    grad_proj_gate = grad_pair_sum[:, :proj_width].astype(f32)
    grad_proj_up = grad_pair_sum[:, proj_width:].astype(f32)

    late = sum_pieces(
        [
            grad_attn_gain,
            grad_attn_shift,
            spread_slot(grad_bias_part[:head_width], tensor, tp_index),
            spread_slot(grad_bias_part[2 * head_width :], tensor, tp_index),
            grad_out_rows,
            grad_mlp_gain,
            grad_mlp_shift,
            grad_fc_out_rows,
            spread_slot(grad_fc_in_part, tensor, tp_index),
            grad_context_gain,
            spread_slot(grad_latent_gain, count, seq_index),
            grad_post_gain,
        ]
    )
    sums = late[4:]
    return (
        latents,
        patches_grad,
        late[0],
        late[1],
        grad_qkv_sum[:, :head_width],
        take_slot(late[2], tensor, tp_index),
        grad_qkv_sum[:, head_width : 2 * head_width],
        grad_qkv_sum[:, 2 * head_width :],
        take_slot(late[3], tensor, tp_index),
        grad_out,
        sums[0],
        sums[1],
        sums[2],
        grad_fc_in,
        take_slot(sums[4], tensor, tp_index),
        grad_fc_out,
        sums[3],
        grad_proj_gate,
        grad_proj_up,
        grad_proj_down,
        grad_latent_param,
        sums[5],
        sums[6],
        grad_res_query,
        grad_res_key,
        grad_res_value,
        grad_res_out,
        sums[7],
        grad_ffn_gate,
        grad_ffn_up,
        grad_ffn_down,
    )


def solution(mesh):
    return jax.shard_map(
        shards,
        mesh=mesh,
        in_specs=(
            P(("seq", "tp"), None),
            P("seq"),
            P(),
            P(),
            P("seq", "tp"),
            P("tp"),
            P("seq", "tp"),
            P("seq", "tp"),
            P("tp"),
            P("tp", "seq"),
            P(),
            P(),
            P(),
            P("seq", "tp"),
            P("tp"),
            P("tp", "seq"),
            P(),
            P("seq", "tp"),
            P("seq", "tp"),
            P("seq", "tp"),
            P("tp", "seq"),
            P(),
            P(),
            P("seq", "tp"),
            P("seq", "tp"),
            P("seq", "tp"),
            P("tp", "seq"),
            P(),
            P(("seq", "tp"), None),
            P(("seq", "tp"), None),
            P(("seq", "tp"), None),
            P(("seq", "tp"), None),
        ),
        out_specs=(
            P(("seq", "tp"), None),
            P(("seq", "tp"), None),
            P(),
            P(),
            P("seq", "tp"),
            P("tp"),
            P("seq", "tp"),
            P("seq", "tp"),
            P("tp"),
            P("tp", "seq"),
            P(),
            P(),
            P(),
            P("seq", "tp"),
            P("tp"),
            P("tp", "seq"),
            P(),
            P("seq", "tp"),
            P("seq", "tp"),
            P("seq", "tp"),
            P("tp", "seq"),
            P(),
            P(),
            P("seq", "tp"),
            P("seq", "tp"),
            P("seq", "tp"),
            P("tp", "seq"),
            P(),
            P(("seq", "tp"), None),
            P(("seq", "tp"), None),
            P(("seq", "tp"), None),
        ),
        check_vma=False,
    )
```
